32 devices in a mesh: groups: 2 (over y), head: 16 (over z, x, core).
Axes of the slice: x: 2, y: 2, z: 4, core: 2. Of those that a mesh axis runs over, the one named last changes fastest.
Arguments:
- tokens: bfloat16 [768, 8192], P('groups', 'head'), parts along dimension 0, may hold values from -6 to 6
- segment_ids: int32 [768], P('groups'), parts along dimension 0, may hold values from 0 to 5, never falling along the last dimension, each value on 1 to 96 neighbouring positions
- in_weight: bfloat16 [8192, 8192], P('head'), may hold values from -0.0625 to 0.0625
- dt_weight: bfloat16 [8192, 16], P(None, 'head'), may hold values from -0.0625 to 0.0625
- conv_weight: float32 [4, 6144], P(None, 'head'), may hold values from -3 to 3
- conv_bias: float32 [6144], P('head'), may hold values from -0.5 to 0.5
- a_rate: float32 [16], P('head'), may hold values from 0.003 to 0.1
- dt_bias: float32 [16], P('head'), may hold values from -1.5 to 0.5
- out_weight: bfloat16 [2048, 8192], P(None, 'head'), may hold values from -0.1875 to 0.1875
Outputs:
- mixed_out: bfloat16 [768, 8192], P('groups', 'head'), parts along dimension 0
The draws below stay inside these ranges and needn't reach their ends.
There are 2 independent parts, one for each index of `groups`. The reference program is written for one: setup_inputs(seed, part) draws one part's arguments, and reference() takes and returns one part's arrays. A program takes and returns all parts, laid end to end along the dimension named above; an argument that names none is the same for every part. Nothing has to cross between parts.
Inputs may be any that keep to these rules, and one draw needn't show every extreme that they name: `segment_ids`: never falls along the sequence; each value marks one document of 1 to 96 consecutive positions.
All inputs are finite; a program needn't handle non-finite values.
Results may differ from the reference program's by a relative error of at most 0.0046.
The reference program's roundings to bfloat16 on the way (of `projected` and `normed`) count: a program that leaves them out, or rounds other values in their place, can miss the bound.
Values may be sent and summed in bfloat16 or wider, within the bound.
A program may use at most 128 MiB of HBM per device.

```python
import math
import jax
import jax.numpy as jnp
import numpy as np
from jax import lax

D = 8192
HEAD_DIM = 128
STATE = 128
CONV = 4
SEQ = 384
HEADS = 16


def strengthened(drawn, own_key, source, target, blocks, factor):
    owner, partner = [(jnp.arange(drawn.shape[position]) // (drawn.shape[position] // blocks)).reshape([-1 if axis == position else 1 for axis in range(drawn.ndim)]) for position in (source, target)]
    chosen = jax.random.permutation(own_key, blocks)[partner]
    strong = (owner == chosen) | (owner == (partner + blocks // 2) % blocks)
    return jnp.where(strong, factor * drawn, drawn)


def block_scale(own_key, extent, pieces, smallest, high):
    def one(dim, shards_of):
        steps = jax.random.uniform(jax.random.fold_in(jax.random.fold_in(own_key, 6), dim), (shards_of,), jnp.float32, smallest / len(pieces), high / len(pieces))
        return jnp.repeat(jnp.exp(steps), extent[dim] // shards_of).reshape((-1,) + (1,) * (len(extent) - dim - 1))

    factor_of = one(*pieces[0])
    for cut in pieces[1:]:
        factor_of = factor_of * one(*cut)
    return factor_of


def profile(number_of, total, bound, slope):
    portions = [(1 << 20) // math.isqrt(rank ** slope) + 1 for rank in range(2, number_of + 1)]
    spare, holding = total - bound - (number_of - 1), [1] * (number_of - 1)
    while spare > 0:
        movable = [i for i in range(number_of - 1) if holding[i] < bound]
        pool, left = sum([portions[i] for i in movable]), spare
        for i in movable:
            extra = min(bound - holding[i], max(1, left * portions[i] // pool), spare)
            holding[i] = holding[i] + extra
            spare = spare - extra
    return np.array([bound] + holding)


def ragged_sizes(own_key, number_of, total, most, slope):
    if number_of == 2:
        one = jax.random.randint(own_key, (), max(1, total - most), min(most, total - 1) + 1)
        return jnp.stack([one, total - one])
    tallies = jnp.asarray(profile(number_of, total, most, slope), jnp.int32)
    pairs = (number_of - 1) // 2
    giver, sink = tallies[1:1 + 2 * pairs:2], tallies[2:2 + 2 * pairs:2]
    slack = jnp.minimum(giver - 1, most - sink)
    passed = jax.random.randint(jax.random.fold_in(own_key, 1), (pairs,), 0, 1 << 20) % (slack + 1)
    tallies = tallies.at[1:1 + 2 * pairs:2].set(giver - passed).at[2:2 + 2 * pairs:2].set(sink + passed)
    return tallies[jax.random.permutation(jax.random.fold_in(own_key, 2), number_of)]


def gaussian(rng, shape, deviation, bound, cuts=(), held_as=jnp.bfloat16):
    drawn = deviation * jax.random.normal(rng, shape, jnp.float32)
    if cuts:
        drawn = drawn * block_scale(rng, shape, cuts, -0.22, 0.18)
    return jnp.clip(drawn, -bound, bound).astype(held_as)


def noise_with(stream_key, extent, deviation, most, split, heavy, kind=jnp.bfloat16):
    values = deviation * jax.random.normal(stream_key, extent, jnp.float32)
    if split:
        values = values * block_scale(stream_key, extent, split, -0.22, 0.18)
    return jnp.clip(strengthened(values, jax.random.fold_in(stream_key, 3), *heavy), -most, most).astype(kind)


def setup_inputs(seed: int = 0, part: int = 0) -> dict:
    keys = jax.random.split(jax.random.key(seed), 10)
    part_keys = jax.random.split(jax.random.fold_in(keys[9], part), 10)
    return {
        "tokens": gaussian(part_keys[0], (SEQ, D), 1.0, 6.0, ((1, 16),)),
        "segment_ids": jnp.searchsorted(jnp.cumsum(ragged_sizes(part_keys[1], 6, SEQ, SEQ // 4, 0)), jnp.arange(SEQ), side="right").astype(jnp.int32),
        "in_weight": gaussian(keys[2], (D, HEADS * (2 * HEAD_DIM + 2 * STATE)), D ** -0.5, 0.0625, ((0, 16),)),
        "dt_weight": gaussian(keys[3], (D, HEADS), D ** -0.5, 0.0625, ((1, 16),)),
        "conv_weight": gaussian(keys[4], (CONV, HEADS * (HEAD_DIM + 2 * STATE)), 0.5, 3.0, ((1, 16),), jnp.float32),
        "conv_bias": jnp.clip(jax.random.uniform(keys[5], (HEADS * (HEAD_DIM + 2 * STATE),), jnp.float32, -0.5, 0.5) * block_scale(keys[5], (HEADS * (HEAD_DIM + 2 * STATE),), ((0, 16),), -0.4, 0.0), -0.5, 0.5),
        "a_rate": jnp.clip(jnp.exp(math.log(0.1) - 3.506558 * jax.random.uniform(keys[6], (HEADS,), jnp.float32) ** block_scale(keys[6], (HEADS,), ((0, 16),), -0.2, 0.2)), 0.003, 0.1),
        "dt_bias": jnp.clip(-1.5 + 2.0 * jax.random.uniform(keys[7], (HEADS,), jnp.float32) ** block_scale(keys[7], (HEADS,), ((0, 16),), -0.2, 0.2), -1.5, 0.5),
        "out_weight": noise_with(keys[8], (HEADS * HEAD_DIM, D), (HEADS * HEAD_DIM) ** -0.5, 0.1875, ((1, 16),), (0, 1, 16, 2.0)),
    }


def causal_mix(conv_in, segment_ids, conv_weight, conv_bias):
    positions = conv_in.shape[0]
    running = conv_bias[None, :] + conv_weight[CONV - 1][None, :] * conv_in
    for offset in range(1, CONV):
        earlier = jnp.concatenate([jnp.zeros((offset, conv_in.shape[1]), conv_in.dtype), conv_in[:positions - offset]], axis=0)
        earlier_seg = jnp.concatenate([jnp.full((offset,), -1, jnp.int32), segment_ids[:positions - offset]], axis=0)
        usable = (earlier_seg == segment_ids).astype(conv_in.dtype)
        running = running + conv_weight[CONV - 1 - offset][None, :] * earlier * usable[:, None]
    return jax.nn.silu(running)

def reference(tokens, segment_ids, in_weight, dt_weight, conv_weight, conv_bias, a_rate, dt_bias, out_weight):
    proj_width = 2 * HEAD_DIM + 2 * STATE
    conv_chan = HEAD_DIM + 2 * STATE
    projected = jnp.dot(tokens, in_weight, preferred_element_type=jnp.float32).astype(jnp.bfloat16)
    projected = lax.optimization_barrier(projected).astype(jnp.float32).reshape(SEQ, HEADS, proj_width)
    gate_part = projected[:, :, HEAD_DIM:2 * HEAD_DIM]
    conv_in = jnp.concatenate([projected[:, :, :HEAD_DIM], projected[:, :, 2 * HEAD_DIM:]], axis=2).reshape(SEQ, HEADS * conv_chan)
    conv_out = causal_mix(conv_in, segment_ids, conv_weight, conv_bias).reshape(SEQ, HEADS, conv_chan)
    x_part = conv_out[:, :, :HEAD_DIM]
    b_part = conv_out[:, :, HEAD_DIM:HEAD_DIM + STATE]
    c_part = conv_out[:, :, HEAD_DIM + STATE:]
    step_size = jax.nn.softplus(jnp.dot(tokens, dt_weight, preferred_element_type=jnp.float32) + dt_bias[None, :])
    continues = jnp.concatenate([jnp.zeros((1,), jnp.float32), (segment_ids[1:] == segment_ids[:-1]).astype(jnp.float32)])
    retain = continues[:, None] * jnp.exp(-a_rate[None, :] * step_size)

    def advance(carried, inputs):
        retain_now, step_now, x_now, b_now, c_now = inputs
        carried = retain_now[:, None, None] * carried + (step_now[:, None] * x_now)[:, :, None] * b_now[:, None, :]
        output = jnp.einsum('hpn,hn->hp', carried, c_now, precision=lax.Precision.HIGHEST)
        return (carried, output)
    zero_state = jnp.zeros((HEADS, HEAD_DIM, STATE), jnp.float32)
    _, ssd_out = lax.scan(advance, zero_state, (retain, step_size, x_part, b_part, c_part))
    gated = ssd_out * jax.nn.silu(gate_part)
    normed = (gated * lax.rsqrt(lax.optimization_barrier(jnp.mean(gated * gated, axis=2, keepdims=True)) + 1e-05)).astype(jnp.bfloat16)
    return jnp.dot(normed.reshape(SEQ, HEADS * HEAD_DIM), out_weight, preferred_element_type=jnp.float32).astype(jnp.bfloat16)
```

```python
import jax
import jax.numpy as jnp
from jax import lax
from jax.sharding import PartitionSpec as P

HEAD_DIM = 128
STATE = 128
CONV = 4
BLOCK = 128


def causal_mix(conv_in, segment_ids, conv_weight, conv_bias):
    positions = conv_in.shape[0]
    running = conv_bias[None, :] + conv_weight[CONV - 1][None, :] * conv_in
    for offset in range(1, CONV):
        earlier = jnp.concatenate(
            [jnp.zeros((offset, conv_in.shape[1]), conv_in.dtype), conv_in[: positions - offset]],
            axis=0,
        )
        earlier_seg = jnp.concatenate(
            [jnp.full((offset,), -1, jnp.int32), segment_ids[: positions - offset]], axis=0
        )
        usable = (earlier_seg == segment_ids).astype(conv_in.dtype)
        running = running + conv_weight[CONV - 1 - offset][None, :] * earlier * usable[:, None]
    return jax.nn.silu(running)


def block_scan(x_part, b_part, c_part, step_size, a_rate, segment_ids):
    length, heads_here, _ = x_part.shape
    blocks_count = length // BLOCK
    top = lax.Precision.HIGHEST
    log_decay = (-a_rate[None, :] * step_size).reshape(blocks_count, BLOCK, heads_here)
    cumulative = jnp.cumsum(log_decay, axis=1)
    seg_blocks = segment_ids.reshape(blocks_count, BLOCK)
    x_scaled = (x_part * step_size[:, :, None]).reshape(blocks_count, BLOCK, heads_here, HEAD_DIM)
    b_blocks = b_part.reshape(blocks_count, BLOCK, heads_here, STATE)
    c_blocks = c_part.reshape(blocks_count, BLOCK, heads_here, STATE)
    within = jnp.arange(BLOCK)
    causal = within[:, None] >= within[None, :]
    allowed = (causal[None] & (seg_blocks[:, :, None] == seg_blocks[:, None, :]))[..., None]
    log_gap = cumulative[:, :, None, :] - cumulative[:, None, :, :]
    weights = jnp.where(allowed, jnp.exp(jnp.where(allowed, log_gap, 0.0)), 0.0)
    scores = jnp.einsum("kthn,kshn->ktsh", c_blocks, b_blocks, precision=top)
    y_inner = jnp.einsum("ktsh,kshp->kthp", scores * weights, x_scaled, precision=top)
    last_seg = seg_blocks[:, -1]
    end_weight = (
        jnp.exp(cumulative[:, -1:, :] - cumulative)
        * (seg_blocks == last_seg[:, None]).astype(jnp.float32)[:, :, None]
    )
    local_state = jnp.einsum(
        "kshp,kshn->khpn", x_scaled * end_weight[..., None], b_blocks, precision=top
    )
    prev_seg = jnp.concatenate([jnp.full((1,), -1, jnp.int32), last_seg[:-1]])
    through = (last_seg == prev_seg).astype(jnp.float32)[:, None] * jnp.exp(cumulative[:, -1, :])

    def pass_on(carried, inputs):
        through_block, local_block = inputs
        return (through_block[:, None, None] * carried + local_block, carried)

    zero_state = jnp.zeros((heads_here, HEAD_DIM, STATE), jnp.float32)
    _, entering = lax.scan(pass_on, zero_state, (through, local_state))
    reaches = (seg_blocks == prev_seg[:, None]).astype(jnp.float32)[:, :, None] * jnp.exp(
        cumulative
    )
    y_carry = reaches[..., None] * jnp.einsum("kthn,khpn->kthp", c_blocks, entering, precision=top)
    return (y_inner + y_carry).reshape(length, heads_here, HEAD_DIM)


def body(
    tokens, segment_ids, in_weight, dt_weight, conv_weight, conv_bias, a_rate, dt_bias, out_weight
):
    length = tokens.shape[0]
    heads_here = dt_weight.shape[1]
    proj_width = 2 * HEAD_DIM + 2 * STATE
    conv_chan = HEAD_DIM + 2 * STATE
    dt_rows = lax.all_to_all(dt_weight, "head", split_axis=0, concat_axis=1, tiled=True)
    proj_part = jnp.dot(tokens, in_weight, preferred_element_type=jnp.float32)
    step_part = jnp.dot(tokens, dt_rows, preferred_element_type=jnp.float32)
    proj_sum = lax.psum_scatter(proj_part, "head", scatter_dimension=1, tiled=True)
    step_sum = lax.psum_scatter(step_part, "head", scatter_dimension=1, tiled=True)
    projected = (
        lax.optimization_barrier(proj_sum.astype(jnp.bfloat16))
        .astype(jnp.float32)
        .reshape(length, heads_here, proj_width)
    )
    gate_part = projected[:, :, HEAD_DIM : 2 * HEAD_DIM]
    conv_in = jnp.concatenate(
        [projected[:, :, :HEAD_DIM], projected[:, :, 2 * HEAD_DIM :]], axis=2
    ).reshape(length, heads_here * conv_chan)
    conv_out = causal_mix(conv_in, segment_ids, conv_weight, conv_bias).reshape(
        length, heads_here, conv_chan
    )
    step_size = jax.nn.softplus(step_sum + dt_bias[None, :])
    ssd_out = block_scan(
        conv_out[:, :, :HEAD_DIM],
        conv_out[:, :, HEAD_DIM : HEAD_DIM + STATE],
        conv_out[:, :, HEAD_DIM + STATE :],
        step_size,
        a_rate,
        segment_ids,
    )
    gated = ssd_out * jax.nn.silu(gate_part)
    normed = (gated * lax.rsqrt(jnp.mean(gated * gated, axis=2, keepdims=True) + 1e-05)).astype(
        jnp.bfloat16
    )
    normed = normed.reshape(length, heads_here * HEAD_DIM)
    all_normed = lax.all_gather(normed, "head", axis=1, tiled=True)
    mixed_out = jnp.dot(all_normed, out_weight, preferred_element_type=jnp.float32)
    return mixed_out.astype(jnp.bfloat16)


def solution(mesh):
    return jax.shard_map(
        body,
        mesh=mesh,
        in_specs=(
            P("groups", "head"),
            P("groups"),
            P("head", None),
            P(None, "head"),
            P(None, "head"),
            P("head"),
            P("head"),
            P("head"),
            P(None, "head"),
        ),
        out_specs=P("groups", "head"),
        check_vma=False,
    )
```

```python
import jax
import jax.numpy as jnp
from jax import lax
from jax.experimental import pallas as pl
from jax.experimental.pallas import tpu as pltpu
from jax.sharding import PartitionSpec as P

HEAD_DIM = 128
STATE = 128
CONV = 4
BLOCK = 128


def causal_mix(conv_in, segment_ids, conv_weight, conv_bias):
    positions = conv_in.shape[0]
    running = conv_bias[None, :] + conv_weight[CONV - 1][None, :] * conv_in
    for offset in range(1, CONV):
        earlier = jnp.concatenate(
            [jnp.zeros((offset, conv_in.shape[1]), conv_in.dtype), conv_in[: positions - offset]],
            axis=0,
        )
        earlier_seg = jnp.concatenate(
            [jnp.full((offset,), -1, jnp.int32), segment_ids[: positions - offset]], axis=0
        )
        usable = (earlier_seg == segment_ids).astype(conv_in.dtype)
        running = running + conv_weight[CONV - 1 - offset][None, :] * earlier * usable[:, None]
    return jax.nn.silu(running)


def block_scan(x_part, b_part, c_part, step_size, a_rate, segment_ids):
    length, heads_here, _ = x_part.shape
    blocks_count = length // BLOCK
    top = lax.Precision.HIGHEST
    log_decay = (-a_rate[None, :] * step_size).reshape(blocks_count, BLOCK, heads_here)
    cumulative = jnp.cumsum(log_decay, axis=1)
    seg_blocks = segment_ids.reshape(blocks_count, BLOCK)
    x_scaled = (x_part * step_size[:, :, None]).reshape(blocks_count, BLOCK, heads_here, HEAD_DIM)
    b_blocks = b_part.reshape(blocks_count, BLOCK, heads_here, STATE)
    c_blocks = c_part.reshape(blocks_count, BLOCK, heads_here, STATE)
    within = jnp.arange(BLOCK)
    causal = within[:, None] >= within[None, :]
    allowed = (causal[None] & (seg_blocks[:, :, None] == seg_blocks[:, None, :]))[..., None]
    log_gap = cumulative[:, :, None, :] - cumulative[:, None, :, :]
    weights = jnp.where(allowed, jnp.exp(jnp.where(allowed, log_gap, 0.0)), 0.0)
    scores = jnp.einsum("kthn,kshn->ktsh", c_blocks, b_blocks, precision=top)
    y_inner = jnp.einsum("ktsh,kshp->kthp", scores * weights, x_scaled, precision=top)
    last_seg = seg_blocks[:, -1]
    end_weight = (
        jnp.exp(cumulative[:, -1:, :] - cumulative)
        * (seg_blocks == last_seg[:, None]).astype(jnp.float32)[:, :, None]
    )
    local_state = jnp.einsum(
        "kshp,kshn->khpn", x_scaled * end_weight[..., None], b_blocks, precision=top
    )
    prev_seg = jnp.concatenate([jnp.full((1,), -1, jnp.int32), last_seg[:-1]])
    through = (last_seg == prev_seg).astype(jnp.float32)[:, None] * jnp.exp(cumulative[:, -1, :])

    def pass_on(carried, inputs):
        through_block, local_block = inputs
        return (through_block[:, None, None] * carried + local_block, carried)

    zero_state = jnp.zeros((heads_here, HEAD_DIM, STATE), jnp.float32)
    _, entering = lax.scan(pass_on, zero_state, (through, local_state))
    reaches = (seg_blocks == prev_seg[:, None]).astype(jnp.float32)[:, :, None] * jnp.exp(
        cumulative
    )
    y_carry = reaches[..., None] * jnp.einsum("kthn,khpn->kthp", c_blocks, entering, precision=top)
    return (y_inner + y_carry).reshape(length, heads_here, HEAD_DIM)


def body(
    tokens, segment_ids, in_weight, dt_weight, conv_weight, conv_bias, a_rate, dt_bias, out_weight
):
    length = tokens.shape[0]
    heads_here = dt_weight.shape[1]
    proj_width = 2 * HEAD_DIM + 2 * STATE
    conv_chan = HEAD_DIM + 2 * STATE
    dt_rows = lax.all_to_all(dt_weight, "head", split_axis=0, concat_axis=1, tiled=True)
    proj_part = jnp.dot(tokens, in_weight, preferred_element_type=jnp.float32)
    step_part = jnp.dot(tokens, dt_rows, preferred_element_type=jnp.float32)
    proj_sum = lax.psum_scatter(proj_part, "head", scatter_dimension=1, tiled=True)
    step_sum = lax.psum_scatter(step_part, "head", scatter_dimension=1, tiled=True)
    projected = (
        lax.optimization_barrier(proj_sum.astype(jnp.bfloat16))
        .astype(jnp.float32)
        .reshape(length, heads_here, proj_width)
    )
    gate_part = projected[:, :, HEAD_DIM : 2 * HEAD_DIM]
    conv_in = jnp.concatenate(
        [projected[:, :, :HEAD_DIM], projected[:, :, 2 * HEAD_DIM :]], axis=2
    ).reshape(length, heads_here * conv_chan)
    conv_out = causal_mix(conv_in, segment_ids, conv_weight, conv_bias).reshape(
        length, heads_here, conv_chan
    )
    step_size = jax.nn.softplus(step_sum + dt_bias[None, :])
    ssd_out = block_scan(
        conv_out[:, :, :HEAD_DIM],
        conv_out[:, :, HEAD_DIM : HEAD_DIM + STATE],
        conv_out[:, :, HEAD_DIM + STATE :],
        step_size,
        a_rate,
        segment_ids,
    )
    gated = ssd_out * jax.nn.silu(gate_part)
    normed = (gated * lax.rsqrt(jnp.mean(gated * gated, axis=2, keepdims=True) + 1e-05)).astype(
        jnp.bfloat16
    )
    normed = normed.reshape(length, heads_here * HEAD_DIM)
    all_normed = lax.all_gather(normed, "head", axis=1, tiled=True)
    mixed_out = jnp.dot(all_normed, out_weight, preferred_element_type=jnp.float32)
    return mixed_out.astype(jnp.bfloat16)


CHUNK = 128
BLOCK_COLS = 2 * HEAD_DIM + 2 * STATE
CODE_STEP = 1170.0
CODE_LOW = 16.0
LN2 = 0.6931471805599453
MESH = pl.DeviceIdType.MESH


def encode(value):
    level = jnp.log(jnp.maximum(jnp.abs(value), 2.0**-CODE_LOW)) * (CODE_STEP / LN2) + CODE_LOW * CODE_STEP
    level = jnp.minimum(jnp.round(level), 32767.0)
    return jnp.where(value < 0, -level, level).astype(jnp.int32).astype(jnp.int16)


def decode(code):
    level = code.astype(jnp.int32).astype(jnp.float32)
    size = jnp.exp(jnp.abs(level) * (LN2 / CODE_STEP) - CODE_LOW * LN2)
    return jnp.where(level < 0, -size, jnp.where(level > 0, size, 0.0))


def fused(
    tok_ref, w_ref, dtw_ref, segc_ref, segr_ref, cw_ref, cb_ref, par_ref, ow_ref, out_ref,
    tok, wbuf, owbuf, dtw, pdt_out, pdt_in, xs, xr, zs, ur, dr, acc, part, conv, gate, gat, state,
    loc_sem, wsend, wrecv, tsem, dws, dwr, pds, pdr, xss, xrs, zss, urs, drs, gsend, grecv,
):
    chunks = tok_ref.shape[0] // CHUNK
    heads = dtw_ref.shape[0]
    depth = tok_ref.shape[1]
    me = lax.axis_index("head")
    core = me % 2
    x = (me // 2) % 2
    z = me // 4
    sib = me + 1 - 2 * core
    xnb = me + 2 - 4 * x
    up_dev = me + 4
    down_dev = me - 4

    def order(k):
        return lax.rem(lax.div(jnp.int32((15, 114, 153, 228)[k]), lax.select(z == 0, 1, lax.select(z == 1, 4, lax.select(z == 2, 16, 64)))), 4)

    def head_of(xx, zz, cc):
        return zz * 4 + xx * 2 + cc

    def remote(src, dst, ss, rs, dev):
        return pltpu.make_async_remote_copy(
            src_ref=src, dst_ref=dst, send_sem=ss, recv_sem=rs, device_id={"head": dev}, device_id_type=MESH
        )

    barrier = pltpu.get_barrier_semaphore()
    for step in range(1, heads):
        pl.semaphore_signal(barrier, inc=1, device_id={"head": lax.rem(me + step, heads)}, device_id_type=MESH)

    def local_w(k, side):
        col = head_of(1 - x if side == 0 else x, order(k), core) * BLOCK_COLS
        slot = side * 4 + k
        return pltpu.make_async_copy(
            w_ref.at[:, pl.ds(pl.multiple_of(col, BLOCK_COLS), BLOCK_COLS)], wbuf.at[slot, pl.ds(0, depth)], loc_sem.at[slot]
        )

    def sib_w(k, side):
        col = head_of(1 - x if side == 0 else x, order(k), 1 - core) * BLOCK_COLS
        slot = side * 4 + k
        return remote(
            w_ref.at[:, pl.ds(pl.multiple_of(col, BLOCK_COLS), BLOCK_COLS)],
            wbuf.at[slot, pl.ds(depth, depth)], wsend.at[slot], wrecv.at[slot], sib,
        )

    pairs = [(k, side) for side in range(2) for k in range(4)]
    local_tok = pltpu.make_async_copy(tok_ref, tok.at[0], loc_sem.at[8])
    local_tok.start()
    for k, side in pairs:
        local_w(k, side).start()
    local_ow = pltpu.make_async_copy(ow_ref, owbuf, loc_sem.at[9])
    local_ow.start()
    pl.semaphore_wait(barrier, heads - 1)

    sib_tok = remote(tok_ref, tok.at[1], tsem.at[0], tsem.at[1], sib)
    sib_tok.start()
    for k, side in pairs:
        sib_w(k, side).start()

    def dtw_copy(step, incoming):
        other = lax.rem(me + step, heads)
        return remote(dtw_ref.at[other], dtw.at[other if incoming else me], dws.at[step], dwr.at[heads - step if incoming else step], other)

    for step in range(1, heads):
        dtw_copy(step, False).start()
    own_dtw = pltpu.make_async_copy(dtw_ref.at[me], dtw.at[me], loc_sem.at[10])
    own_dtw.start()
    local_tok.wait()
    sib_tok.wait_recv()

    def product(slot, r):
        rows = pl.ds(r * CHUNK, CHUNK)
        return jnp.dot(tok[0, rows, :], wbuf[slot, :depth], preferred_element_type=jnp.float32) + jnp.dot(
            tok[1, rows, :], wbuf[slot, depth:], preferred_element_type=jnp.float32
        )

    def x_copy(r, k):
        return remote(xs.at[r, k], xr.at[r, k], xss.at[r, k], xrs.at[r, k], xnb)

    def z_copy(r, d, k, buf, sems, dev):
        return remote(zs.at[r, k], buf.at[r, d], zss.at[r, k], sems.at[r, d], dev)

    def x_phase(r):
        for k in range(4):
            if r == 0:
                local_w(k, 0).wait()
                sib_w(k, 0).wait_recv()
            xs[r, k] = encode(product(k, r))
            x_copy(r, k).start()

    def z_phase(r):
        for k in range(4):
            if r == 0:
                local_w(k, 1).wait()
                sib_w(k, 1).wait_recv()
            d = order(k)
            mine = product(4 + k, r)
            x_copy(r, k).wait_recv()
            mine = mine + decode(xr[r, k])
            if k == 3:
                acc[r] = mine
            else:
                part[...] = mine
                for buf, sems, dev, here, first in (
                    (ur, urs, up_dev, d > z, z == 0),
                    (dr, drs, down_dev, d < z, z == 3),
                ):

                    @pl.when(here)
                    def _(buf=buf, sems=sems, dev=dev, first=first):
                        @pl.when(jnp.logical_not(first))
                        def _():
                            z_copy(r, d, k, buf, sems, dev).wait_recv()
                            part[...] += decode(buf[r, d])

                        zs[r, k] = encode(part[...])
                        z_copy(r, d, k, buf, sems, dev).start()

    def pdt_copy(step, incoming):
        other = lax.rem(me + step, heads)
        return remote(pdt_out.at[other], pdt_in.at[other if incoming else me], pds.at[step], pdr.at[heads - step if incoming else step], other)

    def step_phase():
        own_dtw.wait()
        for step in range(1, heads):
            dtw_copy(step, True).wait_recv()
        total = jnp.zeros((heads, tok_ref.shape[0]), jnp.float32)
        for j in range(depth // 128):
            total = total + lax.dot_general(
                dtw[:, j, :].astype(jnp.bfloat16), tok[0, :, j * 128 : (j + 1) * 128],
                (((1,), (1,)), ((), ())), preferred_element_type=jnp.float32,
            )
        for r in range(chunks):
            pdt_out[:, r, :] = total[:, r * CHUNK : (r + 1) * CHUNK]
        for r in range(chunks, 8):
            pdt_out[:, r, :] = jnp.zeros((heads, 128), jnp.float32)
        for step in range(1, heads):
            pdt_copy(step, False).start()
        own = pltpu.make_async_copy(pdt_out.at[me], pdt_in.at[me], loc_sem.at[11])
        own.start()
        own.wait()

    top = lax.Precision.HIGHEST

    def dot32(a, b, dims):
        return lax.dot_general(a, b, (dims, ((), ())), precision=top, preferred_element_type=jnp.float32)

    def block_phase(r):
        for edge, buf, sems, dev in ((0, ur, urs, up_dev), (3, dr, drs, down_dev)):

            @pl.when(z != edge)
            def _(buf=buf, sems=sems, dev=dev):
                z_copy(r, z, 3, buf, sems, dev).wait_recv()
                acc[r] += decode(buf[r, z])

        gate[...] = acc[r].astype(jnp.bfloat16)
        projected = gate[...].astype(jnp.float32)
        base = 8 + r * CHUNK
        conv[base : base + CHUNK, :HEAD_DIM] = projected[:, :HEAD_DIM]
        conv[base : base + CHUNK, HEAD_DIM:] = projected[:, 2 * HEAD_DIM :]
        gate_part = projected[:, HEAD_DIM : 2 * HEAD_DIM]
        seg_col = segc_ref[base : base + CHUNK, :]
        seg_row = segr_ref[:, r * CHUNK : (r + 1) * CHUNK]
        running = cb_ref[...] + cw_ref[CONV - 1 : CONV, :] * conv[base : base + CHUNK, :]
        for offset in range(1, CONV):
            usable = (segc_ref[base - offset : base - offset + CHUNK, :] == seg_col).astype(jnp.float32)
            running = running + cw_ref[CONV - 1 - offset : CONV - offset, :] * conv[base - offset : base - offset + CHUNK, :] * usable
        conv_out = running / (1.0 + jnp.exp(-running))
        x_part = conv_out[:, :HEAD_DIM]
        b_part = conv_out[:, HEAD_DIM : HEAD_DIM + STATE]
        c_part = conv_out[:, HEAD_DIM + STATE :]

        raw = jnp.sum(pdt_in[:, r, :], axis=0, keepdims=True) + par_ref[1:2, :]
        step_row = jnp.maximum(raw, 0.0) + jnp.log1p(jnp.exp(-jnp.abs(raw)))
        decay_row = -par_ref[0:1, :] * step_row
        t_at = lax.broadcasted_iota(jnp.int32, (CHUNK, CHUNK), 0)
        s_at = lax.broadcasted_iota(jnp.int32, (CHUNK, CHUNK), 1)
        step_col = jnp.sum(jnp.where(t_at == s_at, step_row, 0.0), axis=1, keepdims=True)
        cum_col = jnp.sum(jnp.where(t_at >= s_at, decay_row, 0.0), axis=1, keepdims=True)
        cum_row = jnp.sum(jnp.where(t_at == s_at, cum_col, 0.0), axis=0, keepdims=True)
        allowed = (t_at >= s_at) & (seg_col == seg_row)
        weights = jnp.where(allowed, jnp.exp(jnp.where(allowed, cum_col - cum_row, 0.0)), 0.0)
        x_scaled = x_part * step_col
        scores = dot32(c_part, b_part, ((1,), (1,)))
        y = dot32(scores * weights, x_scaled, ((1,), (0,)))
        last_seg = segc_ref[base + CHUNK - 1 : base + CHUNK, :]
        cum_last = cum_col[CHUNK - 1 : CHUNK, :]
        if r > 0:
            prev_seg = segc_ref[base - 1 : base, :]
            reaches = (seg_col == prev_seg).astype(jnp.float32) * jnp.exp(cum_col)
            y = y + reaches * dot32(c_part, state[...], ((1,), (1,)))
        if r < chunks - 1:
            end_weight = jnp.exp(cum_last - cum_col) * (seg_col == last_seg).astype(jnp.float32)
            local = dot32(x_scaled * end_weight, b_part, ((0,), (0,)))
            if r == 0:
                state[...] = local
            else:
                state[...] = (last_seg == prev_seg).astype(jnp.float32) * jnp.exp(cum_last) * state[...] + local
        gated = y * (gate_part / (1.0 + jnp.exp(-gate_part)))
        normed = gated * lax.rsqrt(jnp.mean(gated * gated, axis=1, keepdims=True) + 1e-05)
        gat[r, me] = normed.astype(jnp.bfloat16)

    def g_copy(r, origin, route, dev):
        return remote(gat.at[r, origin], gat.at[r, origin], gsend.at[r, route], grecv.at[r, origin], dev)

    def g_first(r):
        g_copy(r, me, 0, xnb).start()
        g_copy(r, me, 1, sib).start()

        @pl.when(z < 3)
        def _():
            g_copy(r, me, 2, up_dev).start()

        @pl.when(z > 0)
        def _():
            g_copy(r, me, 3, down_dev).start()

    def g_relay(r):
        for dist in range(1, 4):
            for route, sign in ((4, -1), (12, 1)):
                origin = me + 4 * sign * dist
                source = z + sign * dist

                @pl.when((source >= 0) & (source <= 3))
                def _(origin=origin, route=route, sign=sign, dist=dist):
                    g_copy(r, origin, 0, xnb).wait_recv()
                    g_copy(r, origin, route + 2 * (dist - 1), xnb).start()
                    g_copy(r, origin, route + 1 + 2 * (dist - 1), sib).start()
                    if sign < 0 and dist < 3:

                        @pl.when(z < 3)
                        def _():
                            g_copy(r, origin, 20 + dist, up_dev).start()

                    if sign > 0 and dist < 3:

                        @pl.when(z > 0)
                        def _():
                            g_copy(r, origin, 23 + dist, down_dev).start()

        for j in range(4):
            origin = head_of(1 - x, j, core)
            g_copy(r, origin, 0, sib).wait_recv()
            g_copy(r, origin, 27 + j, sib).start()

    def g_finish(r):
        for j in range(8):
            g_copy(r, j * 2 + 1 - core, 0, sib).wait_recv()
        total = jnp.zeros((CHUNK, out_ref.shape[1]), jnp.float32)
        for h in range(0, heads, 2):
            pair = jnp.concatenate([gat[r, h], gat[r, h + 1]], axis=1)
            total = total + jnp.dot(pair, owbuf[h * HEAD_DIM : (h + 2) * HEAD_DIM, :], preferred_element_type=jnp.float32)
        out_ref[r * CHUNK : (r + 1) * CHUNK, :] = total.astype(out_ref.dtype)

    def drain():
        sib_tok.wait_send()
        for k, side in pairs:
            sib_w(k, side).wait_send()
        for step in range(1, heads):
            dtw_copy(step, False).wait_send()
            pdt_copy(step, False).wait_send()
        for r in range(chunks):
            for k in range(4):
                x_copy(r, k).wait_send()
            for k in range(3):
                z_copy(r, 0, k, ur, urs, up_dev).wait_send()
            for route in (0, 1, 27, 28, 29, 30):
                g_copy(r, me, route, sib).wait_send()

            @pl.when(z < 3)
            def _():
                g_copy(r, me, 2, sib).wait_send()

            @pl.when(z > 0)
            def _():
                g_copy(r, me, 3, sib).wait_send()

            for dist in range(1, 4):
                for route, sign in ((4, -1), (12, 1)):
                    source = z + sign * dist

                    @pl.when((source >= 0) & (source <= 3))
                    def _(route=route, sign=sign, dist=dist):
                        g_copy(r, me, route + 2 * (dist - 1), sib).wait_send()
                        g_copy(r, me, route + 1 + 2 * (dist - 1), sib).wait_send()
                        if dist < 3:

                            @pl.when((z < 3) if sign < 0 else (z > 0))
                            def _():
                                g_copy(r, me, (20 if sign < 0 else 23) + dist, sib).wait_send()

    conv[0:8, :] = jnp.zeros((8, conv.shape[1]), jnp.float32)
    x_phase(0)
    step_phase()
    z_phase(0)
    for r in range(1, chunks):
        x_phase(r)
        if r == 1:
            for step in range(1, heads):
                pdt_copy(step, True).wait_recv()
        z_phase(r)
        block_phase(r - 1)
        g_first(r - 1)
        if r > 1:
            g_relay(r - 2)
            if r == 2:
                local_ow.wait()
    block_phase(chunks - 1)
    g_first(chunks - 1)
    g_relay(chunks - 2)
    g_finish(0)
    g_relay(chunks - 1)
    for r in range(1, chunks):
        g_finish(r)
    drain()


def fused_body(
    tokens, segment_ids, in_weight, dt_weight, conv_weight, conv_bias, a_rate, dt_bias, out_weight
):
    heads = 16
    length, depth = tokens.shape
    chunks = length // CHUNK
    dtw = jnp.pad(dt_weight.astype(jnp.float32).reshape(heads, depth // 128, 128), ((0, 0), (0, 8 - depth // 128), (0, 0)))
    segc = jnp.concatenate([jnp.full((8,), -1, jnp.int32), segment_ids]).reshape(length + 8, 1)
    par = jnp.broadcast_to(jnp.concatenate([a_rate, dt_bias])[:, None], (2, 128))
    vm = pl.BlockSpec(memory_space=pltpu.VMEM)
    hbm = pl.BlockSpec(memory_space=pl.ANY)
    dma = pltpu.SemaphoreType.DMA
    piece = (chunks, 4, CHUNK, BLOCK_COLS)
    return pl.pallas_call(
        fused,
        out_shape=jax.ShapeDtypeStruct((length, out_weight.shape[1]), jnp.bfloat16),
        in_specs=[vm, hbm, vm, vm, vm, vm, vm, vm, hbm],
        out_specs=vm,
        scratch_shapes=[
            pltpu.VMEM((2, length, depth), jnp.bfloat16),
            pltpu.VMEM((8, 2 * depth, BLOCK_COLS), jnp.bfloat16),
            pltpu.VMEM(out_weight.shape, jnp.bfloat16),
            pltpu.VMEM((heads, 8, 128), jnp.float32),
            pltpu.VMEM((heads, 8, 128), jnp.float32),
            pltpu.VMEM((heads, 8, 128), jnp.float32),
            pltpu.VMEM(piece, jnp.int16),
            pltpu.VMEM(piece, jnp.int16),
            pltpu.VMEM(piece, jnp.int16),
            pltpu.VMEM(piece, jnp.int16),
            pltpu.VMEM(piece, jnp.int16),
            pltpu.VMEM((chunks, CHUNK, BLOCK_COLS), jnp.float32),
            pltpu.VMEM((CHUNK, BLOCK_COLS), jnp.float32),
            pltpu.VMEM((length + 8, HEAD_DIM + 2 * STATE), jnp.float32),
            pltpu.VMEM((CHUNK, BLOCK_COLS), jnp.bfloat16),
            pltpu.VMEM((chunks, heads, CHUNK, HEAD_DIM), jnp.bfloat16),
            pltpu.VMEM((HEAD_DIM, STATE), jnp.float32),
            dma((12,)), dma((8,)), dma((8,)), dma((2,)),
            dma((heads,)), dma((heads,)), dma((heads,)), dma((heads,)),
            dma((chunks, 4)), dma((chunks, 4)), dma((chunks, 4)), dma((chunks, 4)), dma((chunks, 4)),
            dma((chunks, 32)), dma((chunks, heads)),
        ],
        compiler_params=pltpu.CompilerParams(
            collective_id=0, has_side_effects=True, vmem_limit_bytes=48 * 1024 * 1024
        ),
    )(
        tokens, in_weight, dtw, segc, segment_ids.reshape(1, length),
        conv_weight, conv_bias.reshape(1, -1), par, out_weight,
    )


def solution(mesh):
    return jax.shard_map(
        fused_body if mesh.shape["head"] == 16 else body,
        mesh=mesh,
        in_specs=(
            P("groups", "head"),
            P("groups"),
            P("head", None),
            P(None, "head"),
            P(None, "head"),
            P("head"),
            P("head"),
            P("head"),
            P(None, "head"),
        ),
        out_specs=P("groups", "head"),
        check_vma=False,
    )
```

```python
import jax
import jax.numpy as jnp
from jax import lax
from jax.experimental import pallas as pl
from jax.experimental.pallas import tpu as pltpu
from jax.sharding import PartitionSpec as P

HEAD_DIM = 128
STATE = 128
CONV = 4
BLOCK = 128


def causal_mix(conv_in, segment_ids, conv_weight, conv_bias):
    positions = conv_in.shape[0]
    running = conv_bias[None, :] + conv_weight[CONV - 1][None, :] * conv_in
    for offset in range(1, CONV):
        earlier = jnp.concatenate(
            [jnp.zeros((offset, conv_in.shape[1]), conv_in.dtype), conv_in[: positions - offset]],
            axis=0,
        )
        earlier_seg = jnp.concatenate(
            [jnp.full((offset,), -1, jnp.int32), segment_ids[: positions - offset]], axis=0
        )
        usable = (earlier_seg == segment_ids).astype(conv_in.dtype)
        running = running + conv_weight[CONV - 1 - offset][None, :] * earlier * usable[:, None]
    return jax.nn.silu(running)


def block_scan(x_part, b_part, c_part, step_size, a_rate, segment_ids):
    length, heads_here, _ = x_part.shape
    blocks_count = length // BLOCK
    top = lax.Precision.HIGHEST
    log_decay = (-a_rate[None, :] * step_size).reshape(blocks_count, BLOCK, heads_here)
    cumulative = jnp.cumsum(log_decay, axis=1)
    seg_blocks = segment_ids.reshape(blocks_count, BLOCK)
    x_scaled = (x_part * step_size[:, :, None]).reshape(blocks_count, BLOCK, heads_here, HEAD_DIM)
    b_blocks = b_part.reshape(blocks_count, BLOCK, heads_here, STATE)
    c_blocks = c_part.reshape(blocks_count, BLOCK, heads_here, STATE)
    within = jnp.arange(BLOCK)
    causal = within[:, None] >= within[None, :]
    allowed = (causal[None] & (seg_blocks[:, :, None] == seg_blocks[:, None, :]))[..., None]
    log_gap = cumulative[:, :, None, :] - cumulative[:, None, :, :]
    weights = jnp.where(allowed, jnp.exp(jnp.where(allowed, log_gap, 0.0)), 0.0)
    scores = jnp.einsum("kthn,kshn->ktsh", c_blocks, b_blocks, precision=top)
    y_inner = jnp.einsum("ktsh,kshp->kthp", scores * weights, x_scaled, precision=top)
    last_seg = seg_blocks[:, -1]
    end_weight = (
        jnp.exp(cumulative[:, -1:, :] - cumulative)
        * (seg_blocks == last_seg[:, None]).astype(jnp.float32)[:, :, None]
    )
    local_state = jnp.einsum(
        "kshp,kshn->khpn", x_scaled * end_weight[..., None], b_blocks, precision=top
    )
    prev_seg = jnp.concatenate([jnp.full((1,), -1, jnp.int32), last_seg[:-1]])
    through = (last_seg == prev_seg).astype(jnp.float32)[:, None] * jnp.exp(cumulative[:, -1, :])

    def pass_on(carried, inputs):
        through_block, local_block = inputs
        return (through_block[:, None, None] * carried + local_block, carried)

    zero_state = jnp.zeros((heads_here, HEAD_DIM, STATE), jnp.float32)
    _, entering = lax.scan(pass_on, zero_state, (through, local_state))
    reaches = (seg_blocks == prev_seg[:, None]).astype(jnp.float32)[:, :, None] * jnp.exp(
        cumulative
    )
    y_carry = reaches[..., None] * jnp.einsum("kthn,khpn->kthp", c_blocks, entering, precision=top)
    return (y_inner + y_carry).reshape(length, heads_here, HEAD_DIM)


def body(
    tokens, segment_ids, in_weight, dt_weight, conv_weight, conv_bias, a_rate, dt_bias, out_weight
):
    length = tokens.shape[0]
    heads_here = dt_weight.shape[1]
    proj_width = 2 * HEAD_DIM + 2 * STATE
    conv_chan = HEAD_DIM + 2 * STATE
    dt_rows = lax.all_to_all(dt_weight, "head", split_axis=0, concat_axis=1, tiled=True)
    proj_part = jnp.dot(tokens, in_weight, preferred_element_type=jnp.float32)
    step_part = jnp.dot(tokens, dt_rows, preferred_element_type=jnp.float32)
    proj_sum = lax.psum_scatter(proj_part, "head", scatter_dimension=1, tiled=True)
    step_sum = lax.psum_scatter(step_part, "head", scatter_dimension=1, tiled=True)
    projected = (
        lax.optimization_barrier(proj_sum.astype(jnp.bfloat16))
        .astype(jnp.float32)
        .reshape(length, heads_here, proj_width)
    )
    gate_part = projected[:, :, HEAD_DIM : 2 * HEAD_DIM]
    conv_in = jnp.concatenate(
        [projected[:, :, :HEAD_DIM], projected[:, :, 2 * HEAD_DIM :]], axis=2
    ).reshape(length, heads_here * conv_chan)
    conv_out = causal_mix(conv_in, segment_ids, conv_weight, conv_bias).reshape(
        length, heads_here, conv_chan
    )
    step_size = jax.nn.softplus(step_sum + dt_bias[None, :])
    ssd_out = block_scan(
        conv_out[:, :, :HEAD_DIM],
        conv_out[:, :, HEAD_DIM : HEAD_DIM + STATE],
        conv_out[:, :, HEAD_DIM + STATE :],
        step_size,
        a_rate,
        segment_ids,
    )
    gated = ssd_out * jax.nn.silu(gate_part)
    normed = (gated * lax.rsqrt(jnp.mean(gated * gated, axis=2, keepdims=True) + 1e-05)).astype(
        jnp.bfloat16
    )
    normed = normed.reshape(length, heads_here * HEAD_DIM)
    all_normed = lax.all_gather(normed, "head", axis=1, tiled=True)
    mixed_out = jnp.dot(all_normed, out_weight, preferred_element_type=jnp.float32)
    return mixed_out.astype(jnp.bfloat16)


CHUNKS = ((0, 64), (64, 128), (192, 128), (320, 64))
BLOCK_COLS = 2 * HEAD_DIM + 2 * STATE
CODE_STEP = 1170.0
CODE_LOW = 16.0
LN2 = 0.6931471805599453
MESH = pl.DeviceIdType.MESH


def encode(value):
    level = jnp.log(jnp.maximum(jnp.abs(value), 2.0**-CODE_LOW)) * (CODE_STEP / LN2) + CODE_LOW * CODE_STEP
    level = jnp.minimum(jnp.round(level), 32767.0)
    return jnp.where(value < 0, -level, level).astype(jnp.int32).astype(jnp.int16)


def decode(code):
    level = code.astype(jnp.int32).astype(jnp.float32)
    size = jnp.exp(jnp.abs(level) * (LN2 / CODE_STEP) - CODE_LOW * LN2)
    return jnp.where(level < 0, -size, jnp.where(level > 0, size, 0.0))


def fused(
    tok_ref, w_ref, dtw_ref, small_ref, ow_ref, out_ref,
    tok, wbuf, owbuf, dtw, pdt_out, pdt_in, xs, xr, zs, ur, dr, zs2, ur2, dr2, acc, part, conv, gate, gat, state, small, segc,
    loc_sem, wsend, wrecv, tsem, dws, dwr, pds, pdr, xss, xrs, zss, urs, drs, zss2, urs2, drs2, gsend, grecv,
):
    chunks = len(CHUNKS)
    length = tok_ref.shape[0]
    heads = dtw_ref.shape[0]
    depth = tok_ref.shape[1]
    me = lax.axis_index("head")
    core = me % 2
    x = (me // 2) % 2
    z = me // 4
    sib = me + 1 - 2 * core
    xnb = me + 2 - 4 * x
    up_dev = me + 4
    down_dev = me - 4

    def order(k):
        return lax.rem(lax.div(jnp.int32((15, 114, 153, 228)[k]), lax.select(z == 0, 1, lax.select(z == 1, 4, lax.select(z == 2, 16, 64)))), 4)

    def head_of(xx, zz, cc):
        return zz * 4 + xx * 2 + cc

    def remote(src, dst, ss, rs, dev):
        return pltpu.make_async_remote_copy(
            src_ref=src, dst_ref=dst, send_sem=ss, recv_sem=rs, device_id={"head": dev}, device_id_type=MESH
        )

    barrier = pltpu.get_barrier_semaphore()
    for step in range(1, heads):
        pl.semaphore_signal(barrier, inc=1, device_id={"head": lax.rem(me + step, heads)}, device_id_type=MESH)

    def local_w(k, side):
        col = head_of(1 - x if side == 0 else x, order(k), core) * BLOCK_COLS
        slot = side * 4 + k
        return pltpu.make_async_copy(
            w_ref.at[:, pl.ds(pl.multiple_of(col, BLOCK_COLS), BLOCK_COLS)], wbuf.at[slot, pl.ds(0, depth)], loc_sem.at[slot]
        )

    def sib_w(k, side):
        col = head_of(1 - x if side == 0 else x, order(k), 1 - core) * BLOCK_COLS
        slot = side * 4 + k
        return remote(
            w_ref.at[:, pl.ds(pl.multiple_of(col, BLOCK_COLS), BLOCK_COLS)],
            wbuf.at[slot, pl.ds(depth, depth)], wsend.at[slot], wrecv.at[slot], sib,
        )

    pairs = [(k, side) for k in range(4) for side in range(2)]
    local_tok = pltpu.make_async_copy(tok_ref, tok.at[0], loc_sem.at[8])
    local_tok.start()
    local_small = pltpu.make_async_copy(small_ref, small, loc_sem.at[12])
    local_small.start()
    for k, side in pairs:
        local_w(k, side).start()
    local_ow = pltpu.make_async_copy(ow_ref, owbuf, loc_sem.at[9])
    local_ow.start()
    pl.semaphore_wait(barrier, heads - 1)

    def dtw_copy(step, incoming):
        other = lax.rem(me + step, heads)
        return remote(dtw_ref.at[other], dtw.at[other if incoming else me], dws.at[step], dwr.at[heads - step if incoming else step], other)

    sib_tok = remote(tok_ref, tok.at[1], tsem.at[0], tsem.at[1], sib)
    sib_tok.start()
    for k, side in pairs:
        sib_w(k, side).start()
        if k == 0:
            for step in range(1 + side, heads, 2):
                dtw_copy(step, False).start()

    own_dtw = pltpu.make_async_copy(dtw_ref.at[me], dtw.at[me], loc_sem.at[10])
    own_dtw.start()
    local_tok.wait()
    sib_tok.wait_recv()

    ready = set()

    def product(k, side, r):
        start, size = CHUNKS[r]
        slot = side * 4 + k
        if slot not in ready:
            ready.add(slot)
            local_w(k, side).wait()
            sib_w(k, side).wait_recv()
        rows = pl.ds(start, size)
        return jnp.dot(tok[0, rows, :], wbuf[slot, :depth], preferred_element_type=jnp.float32) + jnp.dot(
            tok[1, rows, :], wbuf[slot, depth:], preferred_element_type=jnp.float32
        )

    def x_copy(r, k):
        rows = pl.ds(0, CHUNKS[r][1])
        return remote(xs.at[r, k, rows], xr.at[r, k, rows], xss.at[r, k], xrs.at[r, k], xnb)

    side_bufs = ((zs2, zss2, ur2, urs2, dr2, drs2), (zs, zss, ur, urs, dr, drs))

    def z_copy(r, d, k, up, side=1):
        rows = pl.ds(0, CHUNKS[r][1])
        out, out_sems, ub, us, db, ds = side_bufs[side]
        buf, sems, dev = (ub, us, up_dev) if up else (db, ds, down_dev)
        return remote(out.at[r, k, rows], buf.at[r, d, rows], out_sems.at[r, k], sems.at[r, d], dev)

    def z_sent(r, k, side=1):
        z_copy(r, 0, k, True, side).wait_send()

    def z_received(r, d, side, up):
        size = CHUNKS[r][1]
        z_copy(r, d, 0, up, side).wait_recv()
        return decode(side_bufs[side][2 if up else 4][r, d, :size])

    def x_step(r, k):
        xs[r, k, : CHUNKS[r][1]] = encode(product(k, 0, r))
        x_copy(r, k).start()

    def x_phase(r):
        for k in range(4):
            x_step(r, k)

    def pass_on(r, k, side, mine):
        size = CHUNKS[r][1]
        d = order(k)
        part[:size] = mine
        for up in (True, False):

            @pl.when((d > z) if up else (d < z))
            def _(up=up):
                @pl.when((z != 0) if up else (z != 3))
                def _():
                    part[:size] += z_received(r, d, side, up)

                side_bufs[side][0][r, k, :size] = encode(part[:size])
                z_copy(r, d, k, up, side).start()

    def arrive(r, side, total, size):
        for up in (True, False):

            @pl.when((z != 0) if up else (z != 3))
            def _(up=up):
                total[:size] += z_received(r, z, side, up)

    def z_phase(r):
        size = CHUNKS[r][1]
        for k in range(4):
            mine = product(k, 1, r)
            x_copy(r, k).wait_recv()
            mine = mine + decode(xr[r, k, :size])
            if k == 3:
                acc[r, :size] = mine
            else:
                pass_on(r, k, 1, mine)

    def z_first_step(k):
        for side in range(2):
            if k < 3:
                pass_on(0, k, side, product(k, side, 0))
            elif side == 1:
                acc[0, : CHUNKS[0][1]] = product(k, 1, 0)

    def z_first_end():
        size = CHUNKS[0][1]
        part[:size] = product(3, 0, 0)
        arrive(0, 0, part, size)
        xs[0, 0, :size] = encode(part[:size])
        x_copy(0, 0).start()

    def pdt_copy(step, incoming):
        other = lax.rem(me + step, heads)
        return remote(pdt_out.at[other], pdt_in.at[other if incoming else me], pds.at[step], pdr.at[heads - step if incoming else step], other)

    def step_phase():
        own_dtw.wait()
        for step in range(1, heads):
            dtw_copy(step, True).wait_recv()
        total = jnp.zeros((heads, tok_ref.shape[0]), jnp.float32)
        for j in range(depth // 128):
            total = total + lax.dot_general(
                dtw[:, j, :].astype(jnp.bfloat16), tok[0, :, j * 128 : (j + 1) * 128],
                (((1,), (1,)), ((), ())), preferred_element_type=jnp.float32,
            )
        pdt_out[...] = jnp.zeros(pdt_out.shape, jnp.float32)
        for r, (start, size) in enumerate(CHUNKS):
            pdt_out[:, r, :size] = total[:, start : start + size]
        for step in range(1, heads):
            pdt_copy(step, False).start()
        own = pltpu.make_async_copy(pdt_out.at[me], pdt_in.at[me], loc_sem.at[11])
        own.start()
        own.wait()

    top = lax.Precision.HIGHEST

    def dot32(a, b, dims):
        return lax.dot_general(a, b, (dims, ((), ())), precision=top, preferred_element_type=jnp.float32)

    def block_phase(r):
        start, CHUNK = CHUNKS[r]
        arrive(r, 1, acc.at[r], CHUNK)
        if r == 0:
            x_copy(0, 0).wait_recv()
            acc[0, :CHUNK] += decode(xr[0, 0, :CHUNK])
        gate[:CHUNK] = acc[r, :CHUNK].astype(jnp.bfloat16)
        projected = gate[:CHUNK].astype(jnp.float32)
        base = 8 + start
        conv[base : base + CHUNK, :HEAD_DIM] = projected[:, :HEAD_DIM]
        conv[base : base + CHUNK, HEAD_DIM:] = projected[:, 2 * HEAD_DIM :]
        gate_part = projected[:, HEAD_DIM : 2 * HEAD_DIM]
        seg_col = segc[base : base + CHUNK, :]
        seg_row = small[5:6, start : start + CHUNK]
        running = small[4:5, :] + small[CONV - 1 : CONV, :] * conv[base : base + CHUNK, :]
        for offset in range(1, CONV):
            usable = (segc[base - offset : base - offset + CHUNK, :] == seg_col).astype(jnp.float32)
            running = running + small[CONV - 1 - offset : CONV - offset, :] * conv[base - offset : base - offset + CHUNK, :] * usable
        conv_out = running / (1.0 + jnp.exp(-running))
        x_part = conv_out[:, :HEAD_DIM]
        b_part = conv_out[:, HEAD_DIM : HEAD_DIM + STATE]
        c_part = conv_out[:, HEAD_DIM + STATE :]

        raw = jnp.sum(pdt_in[:, r, :CHUNK], axis=0, keepdims=True) + small[7:8, :CHUNK]
        step_row = jnp.maximum(raw, 0.0) + jnp.log1p(jnp.exp(-jnp.abs(raw)))
        decay_row = -small[6:7, :CHUNK] * step_row
        t_at = lax.broadcasted_iota(jnp.int32, (CHUNK, CHUNK), 0)
        s_at = lax.broadcasted_iota(jnp.int32, (CHUNK, CHUNK), 1)
        step_col = jnp.sum(jnp.where(t_at == s_at, step_row, 0.0), axis=1, keepdims=True)
        cum_col = jnp.sum(jnp.where(t_at >= s_at, decay_row, 0.0), axis=1, keepdims=True)
        cum_row = jnp.sum(jnp.where(t_at == s_at, cum_col, 0.0), axis=0, keepdims=True)
        allowed = (t_at >= s_at) & (seg_col == seg_row)
        weights = jnp.where(allowed, jnp.exp(jnp.where(allowed, cum_col - cum_row, 0.0)), 0.0)
        x_scaled = x_part * step_col
        scores = dot32(c_part, b_part, ((1,), (1,)))
        y = dot32(scores * weights, x_scaled, ((1,), (0,)))
        last_seg = segc[base + CHUNK - 1 : base + CHUNK, :]
        cum_last = cum_col[CHUNK - 1 : CHUNK, :]
        if r > 0:
            prev_seg = segc[base - 1 : base, :]
            reaches = (seg_col == prev_seg).astype(jnp.float32) * jnp.exp(cum_col)
            y = y + reaches * dot32(c_part, state[...], ((1,), (1,)))
        if r < chunks - 1:
            end_weight = jnp.exp(cum_last - cum_col) * (seg_col == last_seg).astype(jnp.float32)
            local = dot32(x_scaled * end_weight, b_part, ((0,), (0,)))
            if r == 0:
                state[...] = local
            else:
                state[...] = (last_seg == prev_seg).astype(jnp.float32) * jnp.exp(cum_last) * state[...] + local
        gated = y * (gate_part / (1.0 + jnp.exp(-gate_part)))
        normed = gated * lax.rsqrt(jnp.mean(gated * gated, axis=1, keepdims=True) + 1e-05)
        gat[me, start : start + CHUNK] = normed.astype(jnp.bfloat16)

    def g_copy(r, origin, route, dev):
        start, size = CHUNKS[r]
        here = gat.at[origin, pl.ds(start, size)]
        return remote(here, here, gsend.at[r, route], grecv.at[r, origin], dev)

    def column(j):
        return lax.rem(z + j, 4) * 4 + lax.rem(me, 4)

    def g_first(r):
        for j in range(1, 4):
            g_copy(r, me, j, column(j)).start()
        g_copy(r, me, 0, xnb).start()
        g_copy(r, me, 4, sib).start()

    def g_relay(r):
        for j in (1, 3, 2):
            origin = column(j)
            g_copy(r, origin, 0, xnb).wait_recv()
            g_copy(r, origin, 4 + j, xnb).start()
            g_copy(r, origin, 7 + j, sib).start()
        for j in (0, 1, 3, 2):
            origin = column(j) + 2 - 4 * x
            g_copy(r, origin, 0, sib).wait_recv()
            g_copy(r, origin, 11 + j, sib).start()

    def g_finish(r):
        for j in range(8):
            g_copy(r, j * 2 + 1 - core, 0, sib).wait_recv()
        start, size = CHUNKS[r]
        total = jnp.zeros((size, out_ref.shape[1]), jnp.float32)
        for h in range(0, heads, 2):
            pair = jnp.concatenate([gat[h, start : start + size], gat[h + 1, start : start + size]], axis=1)
            total = total + jnp.dot(pair, owbuf[h * HEAD_DIM : (h + 2) * HEAD_DIM, :], preferred_element_type=jnp.float32)
        out_ref[start : start + size, :] = total.astype(out_ref.dtype)

    def drain():
        sib_tok.wait_send()
        for k, side in pairs:
            sib_w(k, side).wait_send()
        for step in range(1, heads):
            dtw_copy(step, False).wait_send()
            pdt_copy(step, False).wait_send()
        for r in range(chunks):
            for k in range(4 if r else 1):
                x_copy(r, k).wait_send()
            for side in range(2 if r == 0 else 1):
                for k in range(3):
                    z_sent(r, k, 0 if side else 1)
            for route in range(15):
                g_copy(r, me, route, sib).wait_send()

    conv[0:8, :] = jnp.zeros((8, conv.shape[1]), jnp.float32)
    local_small.wait()
    segc[0:8, :] = jnp.full((8, 1), -1.0, jnp.float32)
    for start, size in CHUNKS:
        square = lax.broadcasted_iota(jnp.int32, (size, size), 0) == lax.broadcasted_iota(jnp.int32, (size, size), 1)
        segc[8 + start : 8 + start + size, :] = jnp.sum(
            jnp.where(square, small[5:6, start : start + size], 0.0), axis=1, keepdims=True
        )
    x_step(1, 0)
    z_first_step(0)
    x_step(1, 1)
    step_phase()
    x_step(1, 2)
    z_first_step(1)
    x_step(1, 3)
    x_step(2, 0)
    z_first_step(2)
    x_step(2, 1)
    z_first_step(3)
    z_first_end()
    x_step(2, 2)
    x_step(2, 3)
    z_phase(1)
    for step in range(1, heads):
        pdt_copy(step, True).wait_recv()
    block_phase(0)
    g_first(0)
    x_phase(3)
    z_phase(2)
    block_phase(1)
    g_first(1)
    g_relay(0)
    local_ow.wait()
    block_phase(2)
    g_first(2)
    g_relay(1)
    g_finish(0)
    z_phase(3)
    block_phase(3)
    g_first(3)
    g_relay(2)
    g_finish(1)
    g_relay(3)
    g_finish(2)
    g_finish(3)
    drain()


def fused_body(
    tokens, segment_ids, in_weight, dt_weight, conv_weight, conv_bias, a_rate, dt_bias, out_weight
):
    heads = 16
    length, depth = tokens.shape
    chunks = len(CHUNKS)
    dtw = jnp.pad(dt_weight.astype(jnp.float32).reshape(heads, depth // 128, 128), ((0, 0), (0, 8 - depth // 128), (0, 0)))
    lanes = conv_weight.shape[1]
    at = lax.broadcasted_iota(jnp.int32, (8, lanes), 0)
    small = jnp.pad(conv_weight, ((0, 8 - CONV), (0, 0)))
    seg_lanes = jnp.pad(segment_ids, (0, lanes - length)).astype(jnp.float32)
    for row, values in ((4, conv_bias), (5, seg_lanes), (6, a_rate), (7, dt_bias)):
        small = jnp.where(at == row, values[None, :], small)
    vm = pl.BlockSpec(memory_space=pltpu.VMEM)
    hbm = pl.BlockSpec(memory_space=pl.ANY)
    dma = pltpu.SemaphoreType.DMA
    most = max(size for _, size in CHUNKS)
    piece = (chunks, 4, most, BLOCK_COLS)
    first = (1, 4, CHUNKS[0][1], BLOCK_COLS)
    return pl.pallas_call(
        fused,
        out_shape=jax.ShapeDtypeStruct((length, out_weight.shape[1]), jnp.bfloat16),
        in_specs=[hbm, hbm, hbm, hbm, hbm],
        out_specs=vm,
        scratch_shapes=[
            pltpu.VMEM((2, length, depth), jnp.bfloat16),
            pltpu.VMEM((8, 2 * depth, BLOCK_COLS), jnp.bfloat16),
            pltpu.VMEM(out_weight.shape, jnp.bfloat16),
            pltpu.VMEM((heads, 8, 128), jnp.float32),
            pltpu.VMEM((heads, 8, 128), jnp.float32),
            pltpu.VMEM((heads, 8, 128), jnp.float32),
            pltpu.VMEM(piece, jnp.int16),
            pltpu.VMEM(piece, jnp.int16),
            pltpu.VMEM(piece, jnp.int16),
            pltpu.VMEM(piece, jnp.int16),
            pltpu.VMEM(piece, jnp.int16),
            pltpu.VMEM(first, jnp.int16),
            pltpu.VMEM(first, jnp.int16),
            pltpu.VMEM(first, jnp.int16),
            pltpu.VMEM((chunks, most, BLOCK_COLS), jnp.float32),
            pltpu.VMEM((most, BLOCK_COLS), jnp.float32),
            pltpu.VMEM((length + 8, HEAD_DIM + 2 * STATE), jnp.float32),
            pltpu.VMEM((most, BLOCK_COLS), jnp.bfloat16),
            pltpu.VMEM((heads, length, HEAD_DIM), jnp.bfloat16),
            pltpu.VMEM((HEAD_DIM, STATE), jnp.float32),
            pltpu.VMEM((8, lanes), jnp.float32),
            pltpu.VMEM((length + 8, 1), jnp.float32),
            dma((13,)), dma((8,)), dma((8,)), dma((2,)),
            dma((heads,)), dma((heads,)), dma((heads,)), dma((heads,)),
            dma((chunks, 4)), dma((chunks, 4)), dma((chunks, 4)), dma((chunks, 4)), dma((chunks, 4)),
            dma((1, 4)), dma((1, 4)), dma((1, 4)),
            dma((chunks, 16)), dma((chunks, heads)),
        ],
        compiler_params=pltpu.CompilerParams(
            collective_id=0, has_side_effects=True, vmem_limit_bytes=60 * 1024 * 1024
        ),
    )(
        tokens, in_weight, dtw, small, out_weight,
    )


def solution(mesh):
    return jax.shard_map(
        fused_body if mesh.shape["head"] == 16 else body,
        mesh=mesh,
        in_specs=(
            P("groups", "head"),
            P("groups"),
            P("head", None),
            P(None, "head"),
            P(None, "head"),
            P("head"),
            P("head"),
            P("head"),
            P(None, "head"),
        ),
        out_specs=P("groups", "head"),
        check_vma=False,
    )
```

```python
import jax
import jax.numpy as jnp
from jax import lax
from jax.experimental import pallas as pl
from jax.experimental.pallas import tpu as pltpu
from jax.sharding import PartitionSpec as P

HEAD_DIM = 128
STATE = 128
CONV = 4
BLOCK = 128


def causal_mix(conv_in, segment_ids, conv_weight, conv_bias):
    positions = conv_in.shape[0]
    running = conv_bias[None, :] + conv_weight[CONV - 1][None, :] * conv_in
    for offset in range(1, CONV):
        earlier = jnp.concatenate(
            [jnp.zeros((offset, conv_in.shape[1]), conv_in.dtype), conv_in[: positions - offset]],
            axis=0,
        )
        earlier_seg = jnp.concatenate(
            [jnp.full((offset,), -1, jnp.int32), segment_ids[: positions - offset]], axis=0
        )
        usable = (earlier_seg == segment_ids).astype(conv_in.dtype)
        running = running + conv_weight[CONV - 1 - offset][None, :] * earlier * usable[:, None]
    return jax.nn.silu(running)


def block_scan(x_part, b_part, c_part, step_size, a_rate, segment_ids):
    length, heads_here, _ = x_part.shape
    blocks_count = length // BLOCK
    top = lax.Precision.HIGHEST
    log_decay = (-a_rate[None, :] * step_size).reshape(blocks_count, BLOCK, heads_here)
    cumulative = jnp.cumsum(log_decay, axis=1)
    seg_blocks = segment_ids.reshape(blocks_count, BLOCK)
    x_scaled = (x_part * step_size[:, :, None]).reshape(blocks_count, BLOCK, heads_here, HEAD_DIM)
    b_blocks = b_part.reshape(blocks_count, BLOCK, heads_here, STATE)
    c_blocks = c_part.reshape(blocks_count, BLOCK, heads_here, STATE)
    within = jnp.arange(BLOCK)
    causal = within[:, None] >= within[None, :]
    allowed = (causal[None] & (seg_blocks[:, :, None] == seg_blocks[:, None, :]))[..., None]
    log_gap = cumulative[:, :, None, :] - cumulative[:, None, :, :]
    weights = jnp.where(allowed, jnp.exp(jnp.where(allowed, log_gap, 0.0)), 0.0)
    scores = jnp.einsum("kthn,kshn->ktsh", c_blocks, b_blocks, precision=top)
    y_inner = jnp.einsum("ktsh,kshp->kthp", scores * weights, x_scaled, precision=top)
    last_seg = seg_blocks[:, -1]
    end_weight = (
        jnp.exp(cumulative[:, -1:, :] - cumulative)
        * (seg_blocks == last_seg[:, None]).astype(jnp.float32)[:, :, None]
    )
    local_state = jnp.einsum(
        "kshp,kshn->khpn", x_scaled * end_weight[..., None], b_blocks, precision=top
    )
    prev_seg = jnp.concatenate([jnp.full((1,), -1, jnp.int32), last_seg[:-1]])
    through = (last_seg == prev_seg).astype(jnp.float32)[:, None] * jnp.exp(cumulative[:, -1, :])

    def pass_on(carried, inputs):
        through_block, local_block = inputs
        return (through_block[:, None, None] * carried + local_block, carried)

    zero_state = jnp.zeros((heads_here, HEAD_DIM, STATE), jnp.float32)
    _, entering = lax.scan(pass_on, zero_state, (through, local_state))
    reaches = (seg_blocks == prev_seg[:, None]).astype(jnp.float32)[:, :, None] * jnp.exp(
        cumulative
    )
    y_carry = reaches[..., None] * jnp.einsum("kthn,khpn->kthp", c_blocks, entering, precision=top)
    return (y_inner + y_carry).reshape(length, heads_here, HEAD_DIM)


def body(
    tokens, segment_ids, in_weight, dt_weight, conv_weight, conv_bias, a_rate, dt_bias, out_weight
):
    length = tokens.shape[0]
    heads_here = dt_weight.shape[1]
    proj_width = 2 * HEAD_DIM + 2 * STATE
    conv_chan = HEAD_DIM + 2 * STATE
    dt_rows = lax.all_to_all(dt_weight, "head", split_axis=0, concat_axis=1, tiled=True)
    proj_part = jnp.dot(tokens, in_weight, preferred_element_type=jnp.float32)
    step_part = jnp.dot(tokens, dt_rows, preferred_element_type=jnp.float32)
    proj_sum = lax.psum_scatter(proj_part, "head", scatter_dimension=1, tiled=True)
    step_sum = lax.psum_scatter(step_part, "head", scatter_dimension=1, tiled=True)
    projected = (
        lax.optimization_barrier(proj_sum.astype(jnp.bfloat16))
        .astype(jnp.float32)
        .reshape(length, heads_here, proj_width)
    )
    gate_part = projected[:, :, HEAD_DIM : 2 * HEAD_DIM]
    conv_in = jnp.concatenate(
        [projected[:, :, :HEAD_DIM], projected[:, :, 2 * HEAD_DIM :]], axis=2
    ).reshape(length, heads_here * conv_chan)
    conv_out = causal_mix(conv_in, segment_ids, conv_weight, conv_bias).reshape(
        length, heads_here, conv_chan
    )
    step_size = jax.nn.softplus(step_sum + dt_bias[None, :])
    ssd_out = block_scan(
        conv_out[:, :, :HEAD_DIM],
        conv_out[:, :, HEAD_DIM : HEAD_DIM + STATE],
        conv_out[:, :, HEAD_DIM + STATE :],
        step_size,
        a_rate,
        segment_ids,
    )
    gated = ssd_out * jax.nn.silu(gate_part)
    normed = (gated * lax.rsqrt(jnp.mean(gated * gated, axis=2, keepdims=True) + 1e-05)).astype(
        jnp.bfloat16
    )
    normed = normed.reshape(length, heads_here * HEAD_DIM)
    all_normed = lax.all_gather(normed, "head", axis=1, tiled=True)
    mixed_out = jnp.dot(all_normed, out_weight, preferred_element_type=jnp.float32)
    return mixed_out.astype(jnp.bfloat16)


CHUNKS = ((0, 64), (64, 128), (192, 128), (320, 64))
BLOCK_COLS = 2 * HEAD_DIM + 2 * STATE
CODE_STEP = 1170.0
CODE_LOW = 16.0
LN2 = 0.6931471805599453
MESH = pl.DeviceIdType.MESH


def encode(value):
    level = jnp.log(jnp.maximum(jnp.abs(value), 2.0**-CODE_LOW)) * (CODE_STEP / LN2) + CODE_LOW * CODE_STEP
    level = jnp.minimum(jnp.round(level), 32767.0)
    return jnp.where(value < 0, -level, level).astype(jnp.int32).astype(jnp.int16)


def decode(code):
    level = code.astype(jnp.int32).astype(jnp.float32)
    size = jnp.exp(jnp.abs(level) * (LN2 / CODE_STEP) - CODE_LOW * LN2)
    return jnp.where(level < 0, -size, jnp.where(level > 0, size, 0.0))


def fused(
    tok_ref, w_ref, dtw_ref, small_ref, ow_ref, out_ref,
    tok, wbuf, owbuf, dtw, pdt_out, pdt_in, xs, xr, zs, ur, dr, zs2, ur2, dr2, acc, part, conv, gate, gat, state, small, segc,
    loc_sem, wsend, wrecv, tsem, dws, dwr, pds, pdr, xss, xrs, zss, urs, drs, zss2, urs2, drs2, gsend, grecv,
):
    chunks = len(CHUNKS)
    length = tok_ref.shape[0]
    heads = dtw_ref.shape[0]
    depth = tok_ref.shape[1]
    me = lax.axis_index("head")
    core = me % 2
    x = (me // 2) % 2
    z = me // 4
    sib = me + 1 - 2 * core
    xnb = me + 2 - 4 * x
    up_dev = me + 4
    down_dev = me - 4

    def order(k):
        return lax.rem(lax.div(jnp.int32((15, 114, 153, 228)[k]), lax.select(z == 0, 1, lax.select(z == 1, 4, lax.select(z == 2, 16, 64)))), 4)

    def head_of(xx, zz, cc):
        return zz * 4 + xx * 2 + cc

    def remote(src, dst, ss, rs, dev):
        return pltpu.make_async_remote_copy(
            src_ref=src, dst_ref=dst, send_sem=ss, recv_sem=rs, device_id={"head": dev}, device_id_type=MESH
        )

    barrier = pltpu.get_barrier_semaphore()
    for step in range(1, heads):
        pl.semaphore_signal(barrier, inc=1, device_id={"head": lax.rem(me + step, heads)}, device_id_type=MESH)

    def local_w(k, side):
        col = head_of(1 - x if side == 0 else x, order(k), core) * BLOCK_COLS
        slot = side * 4 + k
        return pltpu.make_async_copy(
            w_ref.at[:, pl.ds(pl.multiple_of(col, BLOCK_COLS), BLOCK_COLS)], wbuf.at[slot, pl.ds(0, depth)], loc_sem.at[slot]
        )

    def sib_w(k, side):
        col = head_of(1 - x if side == 0 else x, order(k), 1 - core) * BLOCK_COLS
        slot = side * 4 + k
        return remote(
            w_ref.at[:, pl.ds(pl.multiple_of(col, BLOCK_COLS), BLOCK_COLS)],
            wbuf.at[slot, pl.ds(depth, depth)], wsend.at[slot], wrecv.at[slot], sib,
        )

    pairs = [(k, side) for k in range(4) for side in range(2)]
    local_tok = pltpu.make_async_copy(tok_ref, tok.at[0], loc_sem.at[8])
    local_tok.start()
    local_small = pltpu.make_async_copy(small_ref, small, loc_sem.at[12])
    local_small.start()
    for k, side in pairs:
        local_w(k, side).start()
    local_ow = pltpu.make_async_copy(ow_ref, owbuf, loc_sem.at[9])
    local_ow.start()
    pl.semaphore_wait(barrier, heads - 1)

    def dtw_copy(step, incoming):
        other = lax.rem(me + step, heads)
        return remote(dtw_ref.at[other], dtw.at[other if incoming else me], dws.at[step], dwr.at[heads - step if incoming else step], other)

    sib_tok = remote(tok_ref, tok.at[1], tsem.at[0], tsem.at[1], sib)
    sib_tok.start()
    for k, side in pairs:
        sib_w(k, side).start()
        if k == 0:
            for step in range(1 + side, heads, 2):
                dtw_copy(step, False).start()

    own_dtw = pltpu.make_async_copy(dtw_ref.at[me], dtw.at[me], loc_sem.at[10])
    own_dtw.start()
    local_tok.wait()
    sib_tok.wait_recv()

    ready = set()

    def product(k, side, r):
        start, size = CHUNKS[r]
        slot = side * 4 + k
        if slot not in ready:
            ready.add(slot)
            local_w(k, side).wait()
            sib_w(k, side).wait_recv()
        rows = pl.ds(start, size)
        return jnp.dot(tok[0, rows, :], wbuf[slot, :depth], preferred_element_type=jnp.float32) + jnp.dot(
            tok[1, rows, :], wbuf[slot, depth:], preferred_element_type=jnp.float32
        )

    def x_copy(r, k):
        rows = pl.ds(0, CHUNKS[r][1])
        return remote(xs.at[r, k, rows], xr.at[r, k, rows], xss.at[r, k], xrs.at[r, k], xnb)

    side_bufs = ((zs2, zss2, ur2, urs2, dr2, drs2), (zs, zss, ur, urs, dr, drs))

    def z_copy(r, d, k, up, side=1):
        rows = pl.ds(0, CHUNKS[r][1])
        out, out_sems, ub, us, db, ds = side_bufs[side]
        buf, sems, dev = (ub, us, up_dev) if up else (db, ds, down_dev)
        return remote(out.at[r, k, rows], buf.at[r, d, rows], out_sems.at[r, k], sems.at[r, d], dev)

    def z_sent(r, k, side=1):
        z_copy(r, 0, k, True, side).wait_send()

    def z_received(r, d, side, up):
        size = CHUNKS[r][1]
        z_copy(r, d, 0, up, side).wait_recv()
        return decode(side_bufs[side][2 if up else 4][r, d, :size])

    def x_step(r, k):
        xs[r, k, : CHUNKS[r][1]] = encode(product(k, 0, r))
        x_copy(r, k).start()

    def x_phase(r):
        for k in range(4):
            x_step(r, k)

    def pass_on(r, k, side, mine):
        size = CHUNKS[r][1]
        d = order(k)
        part[:size] = mine
        for up in (True, False):

            @pl.when((d > z) if up else (d < z))
            def _(up=up):
                @pl.when((z != 0) if up else (z != 3))
                def _():
                    part[:size] += z_received(r, d, side, up)

                side_bufs[side][0][r, k, :size] = encode(part[:size])
                z_copy(r, d, k, up, side).start()

    def arrive(r, side, total, size):
        for up in (True, False):

            @pl.when((z != 0) if up else (z != 3))
            def _(up=up):
                total[:size] += z_received(r, z, side, up)

    def z_phase(r):
        size = CHUNKS[r][1]
        for k in range(4):
            mine = product(k, 1, r)
            x_copy(r, k).wait_recv()
            mine = mine + decode(xr[r, k, :size])
            if k == 3:
                acc[r, :size] = mine
            else:
                pass_on(r, k, 1, mine)

    def z_first_step(k):
        for side in range(2):
            if k < 3:
                pass_on(0, k, side, product(k, side, 0))
            elif side == 1:
                acc[0, : CHUNKS[0][1]] = product(k, 1, 0)

    def z_first_end():
        size = CHUNKS[0][1]
        part[:size] = product(3, 0, 0)
        arrive(0, 0, part, size)
        xs[0, 0, :size] = encode(part[:size])
        x_copy(0, 0).start()

    def pdt_copy(step, incoming):
        other = lax.rem(me + step, heads)
        return remote(pdt_out.at[other], pdt_in.at[other if incoming else me], pds.at[step], pdr.at[heads - step if incoming else step], other)

    def step_phase():
        own_dtw.wait()
        for step in range(1, heads):
            dtw_copy(step, True).wait_recv()
        total = jnp.zeros((heads, tok_ref.shape[0]), jnp.float32)
        for j in range(depth // 128):
            total = total + lax.dot_general(
                dtw[:, j, :].astype(jnp.bfloat16), tok[0, :, j * 128 : (j + 1) * 128],
                (((1,), (1,)), ((), ())), preferred_element_type=jnp.float32,
            )
        pdt_out[...] = jnp.zeros(pdt_out.shape, jnp.float32)
        for r, (start, size) in enumerate(CHUNKS):
            pdt_out[:, r, :size] = total[:, start : start + size]
        for step in range(1, heads):
            pdt_copy(step, False).start()
        own = pltpu.make_async_copy(pdt_out.at[me], pdt_in.at[me], loc_sem.at[11])
        own.start()
        own.wait()

    top = lax.Precision.HIGHEST

    def dot32(a, b, dims):
        return lax.dot_general(a, b, (dims, ((), ())), precision=top, preferred_element_type=jnp.float32)

    def block_phase(r):
        start, CHUNK = CHUNKS[r]
        arrive(r, 1, acc.at[r], CHUNK)
        if r == 0:
            x_copy(0, 0).wait_recv()
            acc[0, :CHUNK] += decode(xr[0, 0, :CHUNK])
        gate[:CHUNK] = acc[r, :CHUNK].astype(jnp.bfloat16)
        projected = gate[:CHUNK].astype(jnp.float32)
        base = 8 + start
        conv[base : base + CHUNK, :HEAD_DIM] = projected[:, :HEAD_DIM]
        conv[base : base + CHUNK, HEAD_DIM:] = projected[:, 2 * HEAD_DIM :]
        gate_part = projected[:, HEAD_DIM : 2 * HEAD_DIM]
        seg_col = segc[base : base + CHUNK, :]
        seg_row = small[5:6, start : start + CHUNK]
        running = small[4:5, :] + small[CONV - 1 : CONV, :] * conv[base : base + CHUNK, :]
        for offset in range(1, CONV):
            usable = (segc[base - offset : base - offset + CHUNK, :] == seg_col).astype(jnp.float32)
            running = running + small[CONV - 1 - offset : CONV - offset, :] * conv[base - offset : base - offset + CHUNK, :] * usable
        conv_out = running / (1.0 + jnp.exp(-running))
        x_part = conv_out[:, :HEAD_DIM]
        b_part = conv_out[:, HEAD_DIM : HEAD_DIM + STATE]
        c_part = conv_out[:, HEAD_DIM + STATE :]

        raw = jnp.sum(pdt_in[:, r, :CHUNK], axis=0, keepdims=True) + small[7:8, :CHUNK]
        step_row = jnp.maximum(raw, 0.0) + jnp.log1p(jnp.exp(-jnp.abs(raw)))
        decay_row = -small[6:7, :CHUNK] * step_row
        t_at = lax.broadcasted_iota(jnp.int32, (CHUNK, CHUNK), 0)
        s_at = lax.broadcasted_iota(jnp.int32, (CHUNK, CHUNK), 1)
        step_col = jnp.sum(jnp.where(t_at == s_at, step_row, 0.0), axis=1, keepdims=True)
        cum_col = jnp.sum(jnp.where(t_at >= s_at, decay_row, 0.0), axis=1, keepdims=True)
        cum_row = jnp.sum(jnp.where(t_at == s_at, cum_col, 0.0), axis=0, keepdims=True)
        allowed = (t_at >= s_at) & (seg_col == seg_row)
        weights = jnp.where(allowed, jnp.exp(jnp.where(allowed, cum_col - cum_row, 0.0)), 0.0)
        x_scaled = x_part * step_col
        scores = dot32(c_part, b_part, ((1,), (1,)))
        y = dot32(scores * weights, x_scaled, ((1,), (0,)))
        last_seg = segc[base + CHUNK - 1 : base + CHUNK, :]
        cum_last = cum_col[CHUNK - 1 : CHUNK, :]
        if r > 0:
            prev_seg = segc[base - 1 : base, :]
            reaches = (seg_col == prev_seg).astype(jnp.float32) * jnp.exp(cum_col)
            y = y + reaches * dot32(c_part, state[...], ((1,), (1,)))
        if r < chunks - 1:
            end_weight = jnp.exp(cum_last - cum_col) * (seg_col == last_seg).astype(jnp.float32)
            local = dot32(x_scaled * end_weight, b_part, ((0,), (0,)))
            if r == 0:
                state[...] = local
            else:
                state[...] = (last_seg == prev_seg).astype(jnp.float32) * jnp.exp(cum_last) * state[...] + local
        gated = y * (gate_part / (1.0 + jnp.exp(-gate_part)))
        normed = gated * lax.rsqrt(jnp.mean(gated * gated, axis=1, keepdims=True) + 1e-05)
        gat[me, start : start + CHUNK] = normed.astype(jnp.bfloat16)

    def g_copy(r, origin, route, dev):
        start, size = CHUNKS[r]
        here = gat.at[origin, pl.ds(start, size)]
        return remote(here, here, gsend.at[r, route], grecv.at[r, origin], dev)

    def column(j):
        return lax.rem(z + j, 4) * 4 + lax.rem(me, 4)

    def g_first(r):
        for j in range(1, 4):
            g_copy(r, me, j, column(j)).start()
        g_copy(r, me, 0, xnb).start()
        g_copy(r, me, 4, sib).start()

    def g_relay(r):
        for j in (1, 3, 2):
            origin = column(j)
            g_copy(r, origin, 0, xnb).wait_recv()
            g_copy(r, origin, 4 + j, xnb).start()
            g_copy(r, origin, 7 + j, sib).start()
        for j in (0, 1, 3, 2):
            origin = column(j) + 2 - 4 * x
            g_copy(r, origin, 0, sib).wait_recv()
            g_copy(r, origin, 11 + j, sib).start()

    def g_finish(r):
        for j in range(8):
            g_copy(r, j * 2 + 1 - core, 0, sib).wait_recv()
        start, size = CHUNKS[r]
        total = jnp.zeros((size, out_ref.shape[1]), jnp.float32)
        for h in range(0, heads, 2):
            pair = jnp.concatenate([gat[h, start : start + size], gat[h + 1, start : start + size]], axis=1)
            total = total + jnp.dot(pair, owbuf[h * HEAD_DIM : (h + 2) * HEAD_DIM, :], preferred_element_type=jnp.float32)
        out_ref[start : start + size, :] = total.astype(out_ref.dtype)

    def drain():
        sib_tok.wait_send()
        for k, side in pairs:
            sib_w(k, side).wait_send()
        for step in range(1, heads):
            dtw_copy(step, False).wait_send()
            pdt_copy(step, False).wait_send()
        for r in range(chunks):
            for k in range(4 if r else 1):
                x_copy(r, k).wait_send()
            for side in range(2 if r == 0 else 1):
                for k in range(3):
                    z_sent(r, k, 0 if side else 1)
            for route in range(15):
                g_copy(r, me, route, sib).wait_send()

    conv[0:8, :] = jnp.zeros((8, conv.shape[1]), jnp.float32)
    local_small.wait()
    segc[0:8, :] = jnp.full((8, 1), -1.0, jnp.float32)
    for start, size in CHUNKS:
        square = lax.broadcasted_iota(jnp.int32, (size, size), 0) == lax.broadcasted_iota(jnp.int32, (size, size), 1)
        segc[8 + start : 8 + start + size, :] = jnp.sum(
            jnp.where(square, small[5:6, start : start + size], 0.0), axis=1, keepdims=True
        )
    x_step(1, 0)
    z_first_step(0)
    x_step(1, 1)
    step_phase()
    x_step(1, 2)
    z_first_step(1)
    x_step(1, 3)
    x_step(2, 0)
    z_first_step(2)
    x_step(2, 1)
    z_first_step(3)
    z_first_end()
    x_step(2, 2)
    x_step(2, 3)
    x_phase(3)
    z_phase(1)
    z_phase(2)
    for step in range(1, heads):
        pdt_copy(step, True).wait_recv()
    block_phase(0)
    g_first(0)
    block_phase(1)
    g_first(1)
    z_phase(3)
    g_relay(0)
    block_phase(2)
    g_first(2)
    block_phase(3)
    g_first(3)
    g_relay(1)
    g_relay(2)
    local_ow.wait()
    g_finish(0)
    g_relay(3)
    g_finish(1)
    g_finish(2)
    g_finish(3)
    drain()


def fused_body(
    tokens, segment_ids, in_weight, dt_weight, conv_weight, conv_bias, a_rate, dt_bias, out_weight
):
    heads = 16
    length, depth = tokens.shape
    chunks = len(CHUNKS)
    dtw = jnp.pad(dt_weight.astype(jnp.float32).reshape(heads, depth // 128, 128), ((0, 0), (0, 8 - depth // 128), (0, 0)))
    lanes = conv_weight.shape[1]
    at = lax.broadcasted_iota(jnp.int32, (8, lanes), 0)
    small = jnp.pad(conv_weight, ((0, 8 - CONV), (0, 0)))
    seg_lanes = jnp.pad(segment_ids, (0, lanes - length)).astype(jnp.float32)
    for row, values in ((4, conv_bias), (5, seg_lanes), (6, a_rate), (7, dt_bias)):
        small = jnp.where(at == row, values[None, :], small)
    vm = pl.BlockSpec(memory_space=pltpu.VMEM)
    hbm = pl.BlockSpec(memory_space=pl.ANY)
    dma = pltpu.SemaphoreType.DMA
    most = max(size for _, size in CHUNKS)
    piece = (chunks, 4, most, BLOCK_COLS)
    first = (1, 4, CHUNKS[0][1], BLOCK_COLS)
    return pl.pallas_call(
        fused,
        out_shape=jax.ShapeDtypeStruct((length, out_weight.shape[1]), jnp.bfloat16),
        in_specs=[hbm, hbm, hbm, hbm, hbm],
        out_specs=vm,
        scratch_shapes=[
            pltpu.VMEM((2, length, depth), jnp.bfloat16),
            pltpu.VMEM((8, 2 * depth, BLOCK_COLS), jnp.bfloat16),
            pltpu.VMEM(out_weight.shape, jnp.bfloat16),
            pltpu.VMEM((heads, 8, 128), jnp.float32),
            pltpu.VMEM((heads, 8, 128), jnp.float32),
            pltpu.VMEM((heads, 8, 128), jnp.float32),
            pltpu.VMEM(piece, jnp.int16),
            pltpu.VMEM(piece, jnp.int16),
            pltpu.VMEM(piece, jnp.int16),
            pltpu.VMEM(piece, jnp.int16),
            pltpu.VMEM(piece, jnp.int16),
            pltpu.VMEM(first, jnp.int16),
            pltpu.VMEM(first, jnp.int16),
            pltpu.VMEM(first, jnp.int16),
            pltpu.VMEM((chunks, most, BLOCK_COLS), jnp.float32),
            pltpu.VMEM((most, BLOCK_COLS), jnp.float32),
            pltpu.VMEM((length + 8, HEAD_DIM + 2 * STATE), jnp.float32),
            pltpu.VMEM((most, BLOCK_COLS), jnp.bfloat16),
            pltpu.VMEM((heads, length, HEAD_DIM), jnp.bfloat16),
            pltpu.VMEM((HEAD_DIM, STATE), jnp.float32),
            pltpu.VMEM((8, lanes), jnp.float32),
            pltpu.VMEM((length + 8, 1), jnp.float32),
            dma((13,)), dma((8,)), dma((8,)), dma((2,)),
            dma((heads,)), dma((heads,)), dma((heads,)), dma((heads,)),
            dma((chunks, 4)), dma((chunks, 4)), dma((chunks, 4)), dma((chunks, 4)), dma((chunks, 4)),
            dma((1, 4)), dma((1, 4)), dma((1, 4)),
            dma((chunks, 16)), dma((chunks, heads)),
        ],
        compiler_params=pltpu.CompilerParams(
            collective_id=0, has_side_effects=True, vmem_limit_bytes=60 * 1024 * 1024
        ),
    )(
        tokens, in_weight, dtw, small, out_weight,
    )


def solution(mesh):
    return jax.shard_map(
        fused_body if mesh.shape["head"] == 16 else body,
        mesh=mesh,
        in_specs=(
            P("groups", "head"),
            P("groups"),
            P("head", None),
            P(None, "head"),
            P(None, "head"),
            P("head"),
            P("head"),
            P("head"),
            P(None, "head"),
        ),
        out_specs=P("groups", "head"),
        check_vma=False,
    )
```
